32 devices in a mesh: line: 4 (over y, x), surf: 8 (over z, core).
Axes of the slice: x: 2, y: 2, z: 4, core: 2. Of those that a mesh axis runs over, the one named last changes fastest.
Arguments:
- face_coef: float32 [16, 1024], P('line', 'surf'), may hold values from 0.5 to 2
- face_mix: float32 [16, 17, 17, 1024], P('line', None, None, 'surf'), may hold values from -0.6 to 0.6
- cell_mix: float32 [16, 17, 17, 1024], P('line', None, None, 'surf'), may hold values from -0.6 to 0.6
- time_term: float32 [16, 17, 1024], P('line', None, 'surf'), may hold values from 0.0005 to 1
- couple: float32 [16, 4, 17, 1024], P('line', None, None, 'surf'), may hold values from 0.0005 to 0.05
- rhs: float32 [16, 17, 1024], P('line', None, 'surf'), may hold values from -0.4 to 0.4
- start_delta: float32 [16, 17, 1024], P('line', None, 'surf'), may hold values from -6 to 6
- neighbours: int32 [4, 1024], P(None, 'surf'), may hold values from -1 to 1023, as said below
- wall_type: int32 [1024], P('surf'), may hold values from 0 to 2
Outputs:
- delta: float32 [16, 17, 1024], P('line', None, 'surf')
The draws below stay inside these ranges and needn't reach their ends.
Inputs may be any that keep to these rules, and one draw needn't show every extreme that they name: `neighbours`: -1 marks a missing neighbour. Entries 0 and 1 of a line are -1 or lines of its own grid block (blocks are the aligned runs of 128 lines). Entry 2 is a line of its own block or one of the last 16 lines of the block before it; entry 3 a line of its own block or one of the first 16 lines of the block after it; blocks follow one another cyclically. A line is the neighbour of its neighbour. `wall_type`: 0 slip wall, 1 isothermal wall, 2 catalytic wall.
All inputs are finite; a program needn't handle non-finite values.
Results may differ from the reference program's by a relative error of at most 0.0003.
Values sent between devices are 32-bit elements; how exact they have to be, the bound alone decides.
A program may use at most 64 MiB of HBM per device.

```python
import math
import jax
import jax.numpy as jnp
from jax import lax

NS = 17
BLOCK = 128
COLS = 16
ITERS = 2
NC = 16
LINES = 1024


def draw_neighbours(key, part):
    line_total = LINES
    block_count = LINES // BLOCK
    row_count = BLOCK // COLS
    flips = jax.random.randint(jax.random.fold_in(key, 17), (block_count,), 0, 2)
    global_line = jnp.arange(line_total, dtype=jnp.int32)
    block_of = global_line // BLOCK
    within = global_line % BLOCK
    row_of = within // COLS
    column = within % COLS
    before = jnp.where(column > 0, global_line - 1, -1)
    after = jnp.where(column < COLS - 1, global_line + 1, -1)
    block_prev = (block_of - 1) % block_count
    column_prev = jnp.where(flips[block_prev] == 1, COLS - 1 - column, column)
    down_line = jnp.where(row_of > 0, global_line - COLS, block_prev * BLOCK + (row_count - 1) * COLS + column_prev)
    block_next = (block_of + 1) % block_count
    column_next = jnp.where(flips[block_of] == 1, COLS - 1 - column, column)
    up_line = jnp.where(row_of < row_count - 1, global_line + COLS, block_next * BLOCK + column_next)
    return jnp.stack([before, after, down_line, up_line]).astype(jnp.int32)


def touch_ends(values, own_key, smallest, top_value):
    spot = [jax.random.randint(jax.random.fold_in(own_key, axis), (), 0, length) for axis, length in enumerate(values.shape)]
    widest = values.shape.index(max(values.shape))
    beside = spot[:widest] + [(spot[widest] + 1) % values.shape[widest]] + spot[widest + 1:]
    return values.at[tuple(spot)].set(smallest).at[tuple(beside)].set(top_value)


def block_levels(stream_key, dims, split, least, high):
    level, own = 1.0, jax.random.fold_in(stream_key, 6)
    for position, parts in split:
        steps = jnp.exp(jax.random.uniform(jax.random.fold_in(own, position), (parts,), jnp.float32, least / len(split), high / len(split)))
        level = level * jnp.repeat(steps, dims[position] // parts).reshape([-1 if axis == position else 1 for axis in range(len(dims))])
    return level


def normal_values(key, extent, deviation, limit, shards=(), held_as=jnp.bfloat16):
    level = block_levels(key, extent, shards, -0.22, 0.18) if shards else 1.0
    values = jax.random.normal(key, extent, jnp.float32) * deviation * level
    return jnp.minimum(jnp.maximum(values, -limit), limit).astype(held_as)


def setup_inputs(seed: int = 0) -> dict:
    arg_keys = jax.random.split(jax.random.key(seed), 10)
    face_coef = jnp.clip(jnp.exp(math.log(2.0) - 1.3862944 * jax.random.uniform(arg_keys[0], (NC, LINES), jnp.float32) ** block_levels(arg_keys[0], (NC, LINES), ((0, 4), (1, 8)), -0.2, 0.2)), 0.5, 2.0)
    face_mix = normal_values(arg_keys[1], (NC, NS, NS, LINES), 0.1, 0.6, ((0, 4), (3, 8)), jnp.float32)
    cell_mix = normal_values(arg_keys[2], (NC, NS, NS, LINES), 0.1, 0.6, ((0, 4), (3, 8)), jnp.float32)
    time_term = jnp.clip(jnp.exp(math.log(1.0) - 7.6009024 * jax.random.uniform(arg_keys[3], (NC, NS, LINES), jnp.float32) ** block_levels(arg_keys[3], (NC, NS, LINES), ((0, 4), (2, 8)), -0.2, 0.2)), 0.0005, 1.0)
    couple = jnp.clip(jnp.exp(math.log(0.05) - 4.6051702 * jax.random.uniform(arg_keys[4], (NC, 4, NS, LINES), jnp.float32) ** block_levels(arg_keys[4], (NC, 4, NS, LINES), ((0, 4), (3, 8)), -0.2, 0.2)), 0.0005, 0.05)
    rhs = normal_values(arg_keys[5], (NC, NS, LINES), 0.05, 0.4, ((0, 4), (2, 8)), jnp.float32)
    start_delta = normal_values(arg_keys[6], (NC, NS, LINES), 1.0, 6.0, ((0, 4), (2, 8)), jnp.float32)
    neighbours = draw_neighbours(jax.random.fold_in(arg_keys[9], 71), 0)
    wall_type = touch_ends(jax.random.randint(arg_keys[8], (LINES,), 0, 3), jax.random.fold_in(arg_keys[8], 1), 0, 2).astype(jnp.int32)
    return dict(face_coef=face_coef, face_mix=face_mix, cell_mix=cell_mix, time_term=time_term, couple=couple, rhs=rhs, start_delta=start_delta, neighbours=neighbours, wall_type=wall_type)


wall_levels = (0.5, 4.0, 32.0)

def matrix_product(matrix_left, matrix_right):
    return jnp.einsum('ijb,jkb->ikb', matrix_left, matrix_right, precision=lax.Precision.HIGHEST)

def matrix_vector(matrix_left, vector_right):
    return jnp.einsum('ijb,jb->ib', matrix_left, vector_right, precision=lax.Precision.HIGHEST)

def solve_lines(face_part, mix_part, cell_part, extra_part, wall_part, source_part):
    width = mix_part.shape[1]
    identity = jnp.eye(width, dtype=jnp.float32)[:, :, None]
    coef_below = jnp.concatenate([wall_part[None], face_part[:-1]], 0)
    mix_below = jnp.concatenate([jnp.zeros_like(mix_part[:1]), mix_part[:-1]], 0)
    lower_mask = (jnp.arange(face_part.shape[0]) > 0).astype(jnp.float32)

    def forward_step(state_prev, inputs):
        coupler_prev, solved_prev = state_prev
        coef_up, coef_down, mix_up, mix_down, mix_cell, extra, source, lower_on = inputs
        diagonal = identity * extra[None] + (coef_up + coef_down)[None, None] * identity + mix_cell - jnp.swapaxes(mix_cell, 0, 1)
        lower = lower_on * (-coef_down[None, None] * identity - jnp.swapaxes(mix_down, 0, 1))
        upper = -coef_up[None, None] * identity + mix_up
        schur = diagonal - matrix_product(lower, coupler_prev)
        stacked = jnp.concatenate([upper, (source - matrix_vector(lower, solved_prev))[:, None]], axis=1)
        solved = jnp.linalg.solve(jnp.moveaxis(schur, -1, 0), jnp.moveaxis(stacked, -1, 0))
        solved = jnp.moveaxis(solved, 0, -1)
        coupler_now = solved[:, :width]
        vector_now = solved[:, width]
        return ((coupler_now, vector_now), (coupler_now, vector_now))
    lines_here = source_part.shape[-1]
    zero_matrix = jnp.zeros((width, width, lines_here), jnp.float32)
    zero_vector = jnp.zeros((width, lines_here), jnp.float32)
    inputs = (face_part, coef_below, mix_part, mix_below, cell_part, extra_part, source_part, lower_mask)
    _, (couplers, forward) = lax.scan(forward_step, (zero_matrix, zero_vector), inputs)

    def back_step(above, inputs):
        coupler, vector = inputs
        result = vector - matrix_vector(coupler, above)
        return (result, result)
    _, solution = lax.scan(back_step, zero_vector, (couplers, forward), reverse=True)
    return solution

def reference(face_coef, face_mix, cell_mix, time_term, couple, rhs, start_delta, neighbours, wall_type):
    line_total = rhs.shape[2]
    block_count = line_total // BLOCK
    wall_term = jnp.zeros(wall_type.shape, jnp.float32)
    for wall_kind, wall_value in enumerate(wall_levels):
        wall_term = wall_term + jnp.where(wall_type == wall_kind, wall_value, 0.0).astype(jnp.float32)
    valid_mask = (neighbours >= 0).astype(jnp.float32)
    safe_index = jnp.where(neighbours >= 0, neighbours, 0).astype(jnp.int32)
    diag_extra = time_term + jnp.sum(couple, axis=1)
    weights = couple * valid_mask[None, :, None, :]

    def sweep_once(previous):
        neighbour_vals = jnp.take(previous, safe_index, axis=2)
        right_side = rhs + jnp.sum(weights * jnp.swapaxes(neighbour_vals, 1, 2), axis=1)

        def one_block(block_number):
            start = (block_number * BLOCK).astype(jnp.int32)
            pieces = [lax.dynamic_slice_in_dim(array, start, BLOCK, axis=array.ndim - 1) for array in (face_coef, face_mix, cell_mix, diag_extra, wall_term, right_side)]
            return solve_lines(*pieces)
        solved = lax.map(one_block, jnp.arange(block_count, dtype=jnp.int32))
        return jnp.moveaxis(solved, 0, 2).reshape(right_side.shape)
    previous = start_delta
    for sweep_number in range(ITERS):
        previous = sweep_once(previous)
    return previous
```

```python
import functools

import jax
import jax.numpy as jnp
from jax import lax
from jax.experimental import pallas as pl
from jax.experimental.pallas import tpu as pltpu
from jax.sharding import PartitionSpec as P

ITERS = 2
MESH = pl.DeviceIdType.MESH

wall_levels = (0.5, 4.0, 32.0)


def groups(width, size=6):
    return [range(s, min(s + size, width)) for s in range(0, width, size)]


def product(out, left, right, base=None):
    width = left.shape[0]
    for rows in groups(width):
        acc = [None] * len(rows)
        for j in range(width):
            line = right[j]
            for n, k in enumerate(rows):
                term = left[k, j : j + 1, :] * line
                acc[n] = term if acc[n] is None else acc[n] + term
        for n, k in enumerate(rows):
            out[k] = acc[n] if base is None else base[k] - acc[n]


def invert_in_place(a):
    width = a.shape[0]
    ids = lax.broadcasted_iota(jnp.int32, a.shape[1:], 0)

    def pivot(k, carry):
        inv = 1.0 / a[k, pl.ds(k, 1), :]
        scaled = a[k] * inv
        here = ids == k
        row = jnp.where(here, inv, scaled)
        update = jnp.where(here, 1.0 + inv, scaled)
        for i in range(width):
            a[i] = a[i] - a[i, pl.ds(k, 1), :] * update
        a[k] = row
        return carry

    lax.fori_loop(0, width, pivot, 0)


def matvec(columns, vector):
    width = columns.shape[0]
    parts = [None] * 3
    for j in range(width):
        term = columns[j] * vector[j : j + 1, :]
        parts[j % 3] = term if parts[j % 3] is None else parts[j % 3] + term
    return parts[0] + parts[1] + parts[2]


def kernel(
    n_line, n_surf,
    win, wout, diag, couple, rhs, start, neighbours,
    out,
    dinv, coup, last, mid_inv, work, mat_in, vec_in, x_in, halo, prev, vecs, right, rprime, send_vec, onehot,
    mat_send, mat_recv, vec_send, vec_recv, x_send, x_recv, halo_send, halo_recv,
):
    cells, width, _, lines = diag.shape
    half = n_line // 2
    me = lax.axis_index("line")
    surf = lax.axis_index("surf")
    lower = me < half
    depth = jnp.where(lower, me, n_line - 1 - me)
    inner = jnp.where(lower, me + 1, me - 1)
    outer = jnp.where(lower, lax.rem(me + n_line - 1, n_line), lax.rem(me + 1, n_line))
    is_mid = depth == half - 1
    not_end = depth > 0
    before = lax.rem(surf + n_surf - 1, n_surf)
    after = lax.rem(surf + 1, n_surf)

    barrier = pltpu.get_barrier_semaphore()
    for peer in (inner, outer):
        pl.semaphore_signal(barrier, inc=1, device_id=(peer, surf), device_id_type=MESH)
    for peer in (before, after):
        pl.semaphore_signal(barrier, inc=1, device_id=(me, peer), device_id_type=MESH)
    pl.semaphore_wait(barrier, 4)

    def remote(src, dst, send, recv, device):
        return pltpu.make_async_remote_copy(
            src_ref=src, dst_ref=dst, send_sem=send, recv_sem=recv,
            device_id=device, device_id_type=MESH,
        )

    def halos(src, sweep):
        return (
            remote(src, halo.at[sweep, 0], halo_send.at[sweep, 0], halo_recv.at[sweep, 0], (me, after)),
            remote(src, halo.at[sweep, 1], halo_send.at[sweep, 1], halo_recv.at[sweep, 1], (me, before)),
        )

    first_halos = halos(start, 0)
    for copy in first_halos:
        copy.start()

    source = lax.broadcasted_iota(jnp.int32, (lines, lines), 0)
    own = surf * lines
    for n in range(4):
        onehot[n] = (neighbours[n : n + 1, :] == source + own).astype(jnp.float32)
    onehot[4] = (neighbours[2:3, :] == source + before * lines).astype(jnp.float32)
    onehot[5] = (neighbours[3:4, :] == source + after * lines).astype(jnp.float32)

    mats = remote(last, mat_in.at[0], mat_send.at[0], mat_recv.at[0], (inner, surf))
    mats_mid = remote(last, mat_in.at[1], mat_send.at[1], mat_recv.at[1], (inner, surf))

    @pl.when(not_end)
    def _():
        mats.wait_recv()

    @pl.when(depth == 0)
    def _():
        mat_in[0] = jnp.zeros_like(mat_in[0])

    last[...] = mat_in[0]

    def factor(t, carry):
        product(work, last, win.at[t], diag.at[t])
        dinv[t] = work[...]
        invert_in_place(dinv.at[t])
        product(last, wout.at[t], dinv.at[t])
        coup[t] = last[...]
        return carry

    lax.fori_loop(0, cells, factor, 0)

    @pl.when(jnp.logical_not(is_mid))
    def _():
        mats.start()
        mats.wait_send()

    @pl.when(is_mid)
    def _():
        mats_mid.start()
        mats_mid.wait()
        product(mid_inv, mat_in.at[1], wout.at[cells - 1], work)
        invert_in_place(mid_inv)

    for sweep in range(ITERS):
        if sweep == 0:
            values, copies = start, first_halos
        else:
            values, copies = prev, halos(prev, sweep)
            for copy in copies:
                copy.start()

        def select(vals, which):
            return lax.dot_general(
                vals, onehot[which], (((1,), (0,)), ((), ())),
                precision=lax.Precision.HIGHEST, preferred_element_type=jnp.float32,
            )

        for t in range(cells):
            vals = values[t]
            right[t] = rhs[t] + sum(couple[t, n] * select(vals, n) for n in range(4))
        for copy in copies:
            copy.wait()
        for t in range(cells):
            right[t] = (
                right[t]
                + couple[t, 2] * select(halo[sweep, 0, t], 4)
                + couple[t, 3] * select(halo[sweep, 1, t], 5)
            )

        vec = remote(send_vec, vec_in.at[sweep, 0], vec_send.at[sweep, 0], vec_recv.at[sweep, 0], (inner, surf))
        vec_mid = remote(send_vec, vec_in.at[sweep, 1], vec_send.at[sweep, 1], vec_recv.at[sweep, 1], (inner, surf))

        @pl.when(depth == 0)
        def _():
            vec_in[sweep, 0] = jnp.zeros((width, lines), jnp.float32)

        @pl.when(not_end)
        def _():
            vec.wait_recv()

        send_vec[...] = vec_in[sweep, 0]

        def forward(t, carry):
            rprime[...] = right[t] - matvec(win.at[t], send_vec)
            value = matvec(dinv.at[t], rprime)
            vecs[t] = value
            send_vec[...] = value
            return carry

        lax.fori_loop(0, cells, forward, 0)

        back = remote(vecs.at[0], x_in.at[sweep], x_send.at[sweep], x_recv.at[sweep], (outer, surf))

        @pl.when(jnp.logical_not(is_mid))
        def _():
            vec.start()
            vec.wait_send()
            back.wait_recv()
            vecs[cells - 1] = vecs[cells - 1] - matvec(coup.at[cells - 1], x_in.at[sweep])

        @pl.when(is_mid)
        def _():
            vec_mid.start()
            vec_mid.wait()
            rprime[...] = rprime[...] - matvec(wout.at[cells - 1], vec_in.at[sweep, 1])
            vecs[cells - 1] = matvec(mid_inv, rprime)

        def backward(s, carry):
            t = cells - 2 - s
            vecs[t] = vecs[t] - matvec(coup.at[t], vecs.at[t + 1])
            return carry

        lax.fori_loop(0, cells - 1, backward, 0)

        @pl.when(not_end)
        def _():
            back.start()
            back.wait_send()

        target = out if sweep == ITERS - 1 else prev
        for t in range(cells):
            target[t] = vecs[t]


def on_device(
    face_coef, face_mix, cell_mix, time_term, couple, rhs, start_delta, neighbours, wall_type
):
    cells, width, _, lines = face_mix.shape
    n_line, n_surf = lax.axis_size("line"), lax.axis_size("surf")
    identity = jnp.eye(width, dtype=jnp.float32)[None, :, :, None]
    place = lax.axis_index("line")
    is_first = (place == 0).astype(jnp.float32)
    wall_term = jnp.zeros(wall_type.shape, jnp.float32)
    for wall_kind, wall_value in enumerate(wall_levels):
        wall_term = wall_term + jnp.where(wall_type == wall_kind, wall_value, 0.0)
    below_coef, below_mix = lax.ppermute(
        (face_coef[-1], face_mix[-1]), "line", [(i, i + 1) for i in range(n_line - 1)]
    )
    coef_below = jnp.concatenate([below_coef[None], face_coef[:-1]], 0)
    mix_below = jnp.concatenate([below_mix[None], face_mix[:-1]], 0)
    coef_diag = (coef_below + face_coef).at[0].add(is_first * wall_term)
    extra = time_term + jnp.sum(couple, axis=1) + coef_diag[:, None]
    cell_t = jnp.swapaxes(cell_mix, 1, 2)
    diag_t = identity * extra[:, None] + cell_t - cell_mix
    lower_t = -coef_below[:, None, None] * identity - mix_below
    upper_t = -face_coef[:, None, None] * identity + jnp.swapaxes(face_mix, 1, 2)
    low = place < n_line // 2
    win = jnp.where(low, lower_t, upper_t[::-1])
    wout = jnp.where(low, upper_t, lower_t[::-1])

    def order(array):
        return jnp.where(low, array, array[::-1])

    f32 = jnp.float32
    mat = (width, width, lines)
    vec = (width, lines)
    dma = pltpu.SemaphoreType.DMA
    vmem = pl.BlockSpec(memory_space=pltpu.VMEM)
    solved = pl.pallas_call(
        functools.partial(kernel, n_line, n_surf),
        out_shape=jax.ShapeDtypeStruct((cells,) + vec, f32),
        in_specs=[vmem] * 7,
        out_specs=vmem,
        scratch_shapes=[
            pltpu.VMEM((cells,) + mat, f32),
            pltpu.VMEM((cells,) + mat, f32),
            pltpu.VMEM(mat, f32),
            pltpu.VMEM(mat, f32),
            pltpu.VMEM(mat, f32),
            pltpu.VMEM((2,) + mat, f32),
            pltpu.VMEM((ITERS, 2) + vec, f32),
            pltpu.VMEM((ITERS,) + vec, f32),
            pltpu.VMEM((ITERS, 2, cells) + vec, f32),
            pltpu.VMEM((cells,) + vec, f32),
            pltpu.VMEM((cells,) + vec, f32),
            pltpu.VMEM((cells,) + vec, f32),
            pltpu.VMEM(vec, f32),
            pltpu.VMEM(vec, f32),
            pltpu.VMEM((6, lines, lines), f32),
            dma((2,)), dma((2,)),
            dma((ITERS, 2)), dma((ITERS, 2)),
            dma((ITERS,)), dma((ITERS,)),
            dma((ITERS, 2)), dma((ITERS, 2)),
        ],
        compiler_params=pltpu.CompilerParams(
            collective_id=0, has_side_effects=True, vmem_limit_bytes=40 * 1024 * 1024
        ),
    )(win, wout, order(diag_t), order(couple), order(rhs), order(start_delta), neighbours)
    return order(solved)


def solution(mesh):
    placed = (
        P("line", "surf"),
        P("line", None, None, "surf"),
        P("line", None, None, "surf"),
        P("line", None, "surf"),
        P("line", None, None, "surf"),
        P("line", None, "surf"),
        P("line", None, "surf"),
        P(None, "surf"),
        P("surf"),
    )
    return jax.shard_map(
        on_device, mesh=mesh, in_specs=placed, out_specs=P("line", None, "surf"), check_vma=False
    )
```

```python
import functools

import jax
import jax.numpy as jnp
from jax import lax
from jax.experimental import pallas as pl
from jax.experimental.pallas import tpu as pltpu
from jax.sharding import PartitionSpec as P

ITERS = 2
MESH = pl.DeviceIdType.MESH

wall_levels = (0.5, 4.0, 32.0)


def groups(width, size=6):
    return [range(s, min(s + size, width)) for s in range(0, width, size)]


def product(out, left, right, base=None):
    width = left.shape[0]
    for rows in groups(width):
        acc = [None] * len(rows)
        for j in range(width):
            line = right[j]
            for n, k in enumerate(rows):
                term = left[k, j : j + 1, :] * line
                acc[n] = term if acc[n] is None else acc[n] + term
        for n, k in enumerate(rows):
            out[k] = acc[n] if base is None else base[k] - acc[n]


def invert_in_place(a):
    width = a.shape[0]
    ids = lax.broadcasted_iota(jnp.int32, a.shape[1:], 0)
    rows = [a[i] for i in range(width)]
    for k in range(width):
        inv = 1.0 / rows[k][k : k + 1, :]
        scaled = rows[k] * inv
        here = ids == k
        update = jnp.where(here, 1.0 + inv, scaled)
        for step in range(1, width):
            i = (k + step) % width
            rows[i] = rows[i] - rows[i][k : k + 1, :] * update
        rows[k] = jnp.where(here, inv, scaled)
    for i in range(width):
        a[i] = rows[i]


def matvec(columns, vector):
    width = columns.shape[0]
    parts = [None] * 3
    for j in range(width):
        term = columns[j] * vector[j : j + 1, :]
        parts[j % 3] = term if parts[j % 3] is None else parts[j % 3] + term
    return parts[0] + parts[1] + parts[2]


def kernel(
    n_line, n_surf,
    win_own, wout_own, diag_own, top_mat, top_coef, couple, rhs, start, neighbours,
    out,
    win, wout, diag, edge_mat, edge_coef, edge_send, edge_recv,
    dinv, coup, last, mid_inv, work, mat_in, vec_in, x_in, halo, prev, vecs, right, rprime, send_vec, onehot,
    mat_send, mat_recv, vec_send, vec_recv, x_send, x_recv, halo_send, halo_recv,
):
    cells, width, _, lines = diag_own.shape
    half = n_line // 2
    me = lax.axis_index("line")
    surf = lax.axis_index("surf")
    above = lax.rem(me + 1, n_line)
    below = lax.rem(me + n_line - 1, n_line)
    lower = me < half
    depth = jnp.where(lower, me, n_line - 1 - me)
    inner = jnp.where(lower, me + 1, me - 1)
    outer = jnp.where(lower, lax.rem(me + n_line - 1, n_line), lax.rem(me + 1, n_line))
    is_mid = depth == half - 1
    not_end = depth > 0
    before = lax.rem(surf + n_surf - 1, n_surf)
    after = lax.rem(surf + 1, n_surf)

    barrier = pltpu.get_barrier_semaphore()
    for peer in (above, below):
        pl.semaphore_signal(barrier, inc=1, device_id=(peer, surf), device_id_type=MESH)
    for peer in (before, after):
        pl.semaphore_signal(barrier, inc=1, device_id=(me, peer), device_id_type=MESH)
    pl.semaphore_wait(barrier, 4)

    def remote(src, dst, send, recv, device):
        return pltpu.make_async_remote_copy(
            src_ref=src, dst_ref=dst, send_sem=send, recv_sem=recv,
            device_id=device, device_id_type=MESH,
        )

    def halos(src, sweep):
        return (
            remote(src, halo.at[sweep, 0], halo_send.at[sweep, 0], halo_recv.at[sweep, 0], (me, after)),
            remote(src, halo.at[sweep, 1], halo_send.at[sweep, 1], halo_recv.at[sweep, 1], (me, before)),
        )

    first_halos = halos(start, 0)
    for copy in first_halos:
        copy.start()

    edge_copies = (
        remote(top_mat, edge_mat, edge_send.at[0], edge_recv.at[0], (above, surf)),
        remote(top_coef, edge_coef, edge_send.at[1], edge_recv.at[1], (above, surf)),
    )

    @pl.when(me < n_line - 1)
    def _():
        for copy in edge_copies:
            copy.start()

    source = lax.broadcasted_iota(jnp.int32, (lines, lines), 0)
    own = surf * lines
    for n in range(4):
        onehot[n] = (neighbours[n : n + 1, :] == source + own).astype(jnp.float32)
    onehot[4] = (neighbours[2:3, :] == source + before * lines).astype(jnp.float32)
    onehot[5] = (neighbours[3:4, :] == source + after * lines).astype(jnp.float32)

    mats = remote(last, mat_in.at[0], mat_send.at[0], mat_recv.at[0], (inner, surf))
    mats_mid = remote(last, mat_in.at[1], mat_send.at[1], mat_recv.at[1], (inner, surf))

    @pl.when(not_end)
    def _():
        mats.wait_recv()

    @pl.when(depth == 0)
    def _():
        mat_in[0] = jnp.zeros_like(mat_in[0])

    last[...] = mat_in[0]

    edge_step = jnp.where(lower, 0, cells - 1)
    eye = lax.broadcasted_iota(jnp.int32, (width, lines), 0)

    @pl.when(me == 0)
    def _():
        edge_mat[...] = jnp.zeros_like(edge_mat)
        edge_coef[...] = jnp.zeros_like(edge_coef)

    def factor(t, carry):
        for i in range(width):
            win[t, i] = win_own[t, i]
            wout[t, i] = wout_own[t, i]
            diag[t, i] = diag_own[t, i]

        @pl.when(t == edge_step)
        def _():
            @pl.when(me > 0)
            def _():
                for copy in edge_copies:
                    copy.wait_recv()

            for i in range(width):
                diag[t, i] = diag[t, i] + jnp.where(eye == i, edge_coef[...], 0.0)

            @pl.when(lower)
            def _():
                for i in range(width):
                    win[t, i] = edge_mat[i]

            @pl.when(jnp.logical_not(lower))
            def _():
                for i in range(width):
                    wout[t, i] = edge_mat[i]

        product(work, last, win.at[t], diag.at[t])
        dinv[t] = work[...]
        invert_in_place(dinv.at[t])
        product(last, wout.at[t], dinv.at[t])
        coup[t] = last[...]
        return carry

    lax.fori_loop(0, cells, factor, 0)

    @pl.when(me < n_line - 1)
    def _():
        for copy in edge_copies:
            copy.wait_send()

    @pl.when(jnp.logical_not(is_mid))
    def _():
        mats.start()
        mats.wait_send()

    @pl.when(is_mid)
    def _():
        mats_mid.start()
        mats_mid.wait()
        product(mid_inv, mat_in.at[1], wout.at[cells - 1], work)
        invert_in_place(mid_inv)

    for sweep in range(ITERS):
        if sweep == 0:
            values, copies = start, first_halos
        else:
            values, copies = prev, halos(prev, sweep)
            for copy in copies:
                copy.start()

        def select(vals, which):
            return lax.dot_general(
                vals, onehot[which], (((1,), (0,)), ((), ())),
                precision=lax.Precision.HIGHEST, preferred_element_type=jnp.float32,
            )

        for t in range(cells):
            vals = values[t]
            right[t] = rhs[t] + sum(couple[t, n] * select(vals, n) for n in range(4))
        for copy in copies:
            copy.wait()
        for t in range(cells):
            right[t] = (
                right[t]
                + couple[t, 2] * select(halo[sweep, 0, t], 4)
                + couple[t, 3] * select(halo[sweep, 1, t], 5)
            )

        vec = remote(send_vec, vec_in.at[sweep, 0], vec_send.at[sweep, 0], vec_recv.at[sweep, 0], (inner, surf))
        vec_mid = remote(send_vec, vec_in.at[sweep, 1], vec_send.at[sweep, 1], vec_recv.at[sweep, 1], (inner, surf))

        @pl.when(depth == 0)
        def _():
            vec_in[sweep, 0] = jnp.zeros((width, lines), jnp.float32)

        @pl.when(not_end)
        def _():
            vec.wait_recv()

        send_vec[...] = vec_in[sweep, 0]

        def forward(t, carry):
            rprime[...] = right[t] - matvec(win.at[t], send_vec)
            value = matvec(dinv.at[t], rprime)
            vecs[t] = value
            send_vec[...] = value
            return carry

        lax.fori_loop(0, cells, forward, 0)

        back = remote(vecs.at[0], x_in.at[sweep], x_send.at[sweep], x_recv.at[sweep], (outer, surf))

        @pl.when(jnp.logical_not(is_mid))
        def _():
            vec.start()
            vec.wait_send()
            back.wait_recv()
            vecs[cells - 1] = vecs[cells - 1] - matvec(coup.at[cells - 1], x_in.at[sweep])

        @pl.when(is_mid)
        def _():
            vec_mid.start()
            vec_mid.wait()
            rprime[...] = rprime[...] - matvec(wout.at[cells - 1], vec_in.at[sweep, 1])
            vecs[cells - 1] = matvec(mid_inv, rprime)

        def backward(s, carry):
            t = cells - 2 - s
            vecs[t] = vecs[t] - matvec(coup.at[t], vecs.at[t + 1])
            return carry

        lax.fori_loop(0, cells - 1, backward, 0)

        @pl.when(not_end)
        def _():
            back.start()
            back.wait_send()

        target = out if sweep == ITERS - 1 else prev
        for t in range(cells):
            target[t] = vecs[t]


def on_device(
    face_coef, face_mix, cell_mix, time_term, couple, rhs, start_delta, neighbours, wall_type
):
    cells, width, _, lines = face_mix.shape
    n_line, n_surf = lax.axis_size("line"), lax.axis_size("surf")
    identity = jnp.eye(width, dtype=jnp.float32)[None, :, :, None]
    place = lax.axis_index("line")
    is_first = (place == 0).astype(jnp.float32)
    wall_term = jnp.zeros(wall_type.shape, jnp.float32)
    for wall_kind, wall_value in enumerate(wall_levels):
        wall_term = wall_term + jnp.where(wall_type == wall_kind, wall_value, 0.0)
    coef_diag = face_coef.at[1:].add(face_coef[:-1]).at[0].add(is_first * wall_term)
    extra = time_term + jnp.sum(couple, axis=1) + coef_diag[:, None]
    cell_t = jnp.swapaxes(cell_mix, 1, 2)
    diag_t = identity * extra[:, None] + cell_t - cell_mix
    above_t = -face_coef[:, None, None] * identity - face_mix
    lower_t = jnp.concatenate([jnp.zeros_like(above_t[:1]), above_t[:-1]], 0)
    upper_t = -face_coef[:, None, None] * identity + jnp.swapaxes(face_mix, 1, 2)
    low = place < n_line // 2
    win = jnp.where(low, lower_t, upper_t[::-1])
    wout = jnp.where(low, upper_t, lower_t[::-1])

    def order(array):
        return jnp.where(low, array, array[::-1])

    f32 = jnp.float32
    mat = (width, width, lines)
    vec = (width, lines)
    dma = pltpu.SemaphoreType.DMA
    vmem = pl.BlockSpec(memory_space=pltpu.VMEM)
    solved = pl.pallas_call(
        functools.partial(kernel, n_line, n_surf),
        out_shape=jax.ShapeDtypeStruct((cells,) + vec, f32),
        in_specs=[vmem] * 9,
        out_specs=vmem,
        scratch_shapes=[
            pltpu.VMEM((cells,) + mat, f32),
            pltpu.VMEM((cells,) + mat, f32),
            pltpu.VMEM((cells,) + mat, f32),
            pltpu.VMEM(mat, f32),
            pltpu.VMEM((1, lines), f32),
            dma((2,)), dma((2,)),
            pltpu.VMEM((cells,) + mat, f32),
            pltpu.VMEM((cells,) + mat, f32),
            pltpu.VMEM(mat, f32),
            pltpu.VMEM(mat, f32),
            pltpu.VMEM(mat, f32),
            pltpu.VMEM((2,) + mat, f32),
            pltpu.VMEM((ITERS, 2) + vec, f32),
            pltpu.VMEM((ITERS,) + vec, f32),
            pltpu.VMEM((ITERS, 2, cells) + vec, f32),
            pltpu.VMEM((cells,) + vec, f32),
            pltpu.VMEM((cells,) + vec, f32),
            pltpu.VMEM((cells,) + vec, f32),
            pltpu.VMEM(vec, f32),
            pltpu.VMEM(vec, f32),
            pltpu.VMEM((6, lines, lines), f32),
            dma((2,)), dma((2,)),
            dma((ITERS, 2)), dma((ITERS, 2)),
            dma((ITERS,)), dma((ITERS,)),
            dma((ITERS, 2)), dma((ITERS, 2)),
        ],
        compiler_params=pltpu.CompilerParams(
            collective_id=0, has_side_effects=True, vmem_limit_bytes=40 * 1024 * 1024
        ),
    )(win, wout, order(diag_t), above_t[-1], face_coef[-1:], order(couple), order(rhs), order(start_delta), neighbours)
    return order(solved)


def solution(mesh):
    placed = (
        P("line", "surf"),
        P("line", None, None, "surf"),
        P("line", None, None, "surf"),
        P("line", None, "surf"),
        P("line", None, None, "surf"),
        P("line", None, "surf"),
        P("line", None, "surf"),
        P(None, "surf"),
        P("surf"),
    )
    return jax.shard_map(
        on_device, mesh=mesh, in_specs=placed, out_specs=P("line", None, "surf"), check_vma=False
    )
```

```python
import functools

import jax
import jax.numpy as jnp
from jax import lax
from jax.experimental import pallas as pl
from jax.experimental.pallas import tpu as pltpu
from jax.sharding import PartitionSpec as P

ITERS = 2
MESH = pl.DeviceIdType.MESH

wall_levels = (0.5, 4.0, 32.0)


def groups(width, size=6):
    return [range(s, min(s + size, width)) for s in range(0, width, size)]


def product(out, left, right, base=None):
    width = left.shape[0]
    for rows in groups(width):
        acc = [None] * len(rows)
        for j in range(width):
            line = right[j]
            for n, k in enumerate(rows):
                term = left[k, j : j + 1, :] * line
                acc[n] = term if acc[n] is None else acc[n] + term
        for n, k in enumerate(rows):
            out[k] = acc[n] if base is None else base[k] - acc[n]


def invert_in_place(a):
    width = a.shape[0]
    ids = lax.broadcasted_iota(jnp.int32, a.shape[1:], 0)
    rows = [a[i] for i in range(width)]
    for k in range(width):
        inv = 1.0 / rows[k][k : k + 1, :]
        scaled = rows[k] * inv
        here = ids == k
        update = jnp.where(here, 1.0 + inv, scaled)
        for step in range(1, width):
            i = (k + step) % width
            rows[i] = rows[i] - rows[i][k : k + 1, :] * update
        rows[k] = jnp.where(here, inv, scaled)
    for i in range(width):
        a[i] = rows[i]


def matvec(columns, vector):
    width = columns.shape[0]
    parts = [None] * 3
    for j in range(width):
        term = columns[j] * vector[j : j + 1, :]
        parts[j % 3] = term if parts[j % 3] is None else parts[j % 3] + term
    return parts[0] + parts[1] + parts[2]


def kernel(
    n_line, n_surf,
    win_own, wout_own, diag_own, top_mat, top_coef, couple, rhs, start, neighbours,
    out,
    win, wout, diag, edge_mat, edge_coef, edge_send, edge_recv,
    dinv, coup, last, mid_inv, work, mat_in, vec_in, x_in, halo, prev, vecs, right, rprime, send_vec, onehot, stack, picked,
    mat_send, mat_recv, vec_send, vec_recv, x_send, x_recv, halo_send, halo_recv,
):
    cells, width, _, lines = diag_own.shape
    half = n_line // 2
    rows_each = stack.shape[1] // (3 * cells)
    me = lax.axis_index("line")
    surf = lax.axis_index("surf")
    above = lax.rem(me + 1, n_line)
    below = lax.rem(me + n_line - 1, n_line)
    lower = me < half
    depth = jnp.where(lower, me, n_line - 1 - me)
    inner = jnp.where(lower, me + 1, me - 1)
    outer = jnp.where(lower, lax.rem(me + n_line - 1, n_line), lax.rem(me + 1, n_line))
    is_mid = depth == half - 1
    not_end = depth > 0
    before = lax.rem(surf + n_surf - 1, n_surf)
    after = lax.rem(surf + 1, n_surf)

    barrier = pltpu.get_barrier_semaphore()
    for peer in (above, below):
        pl.semaphore_signal(barrier, inc=1, device_id=(peer, surf), device_id_type=MESH)
    for peer in (before, after):
        pl.semaphore_signal(barrier, inc=1, device_id=(me, peer), device_id_type=MESH)
    pl.semaphore_wait(barrier, 4)

    def remote(src, dst, send, recv, device):
        return pltpu.make_async_remote_copy(
            src_ref=src, dst_ref=dst, send_sem=send, recv_sem=recv,
            device_id=device, device_id_type=MESH,
        )

    def halos(src, sweep):
        return (
            remote(src, halo.at[sweep, 0], halo_send.at[sweep, 0], halo_recv.at[sweep, 0], (me, after)),
            remote(src, halo.at[sweep, 1], halo_send.at[sweep, 1], halo_recv.at[sweep, 1], (me, before)),
        )

    first_halos = halos(start, 0)
    for copy in first_halos:
        copy.start()

    edge_copies = (
        remote(top_mat, edge_mat, edge_send.at[0], edge_recv.at[0], (above, surf)),
        remote(top_coef, edge_coef, edge_send.at[1], edge_recv.at[1], (above, surf)),
    )

    @pl.when(me < n_line - 1)
    def _():
        for copy in edge_copies:
            copy.start()

    source = lax.broadcasted_iota(jnp.int32, (lines, lines), 0)
    own = surf * lines
    for n, (slot, base) in enumerate(
        ((0, own), (1, own), (2, own), (3, own), (2, before * lines), (3, after * lines))
    ):
        hits = neighbours[slot : slot + 1, :] == source + base
        onehot[:, n * lines : (n + 1) * lines] = hits.astype(jnp.float32)
    for which in range(3):
        stack[which] = jnp.zeros_like(stack[which])

    def gather(which, values, first, count):
        pieces = stack.at[which]
        for t in range(cells):
            rest = values[t]
            for q in range(3):
                piece = rest.astype(jnp.bfloat16).astype(jnp.float32)
                begin = (q * cells + t) * rows_each
                pieces[begin : begin + width, :] = piece
                rest = rest - piece
        picked[:, first * lines : (first + count) * lines] = jnp.dot(
            pieces[...].astype(jnp.bfloat16),
            onehot[:, first * lines : (first + count) * lines].astype(jnp.bfloat16),
            preferred_element_type=jnp.float32,
        )

    def chosen(t, n):
        parts = []
        for q in range(3):
            begin = (q * cells + t) * rows_each
            parts.append(picked[begin : begin + width, n * lines : (n + 1) * lines])
        return parts[2] + parts[1] + parts[0]

    def form_right(values, copies, sweep):
        gather(0, values, 0, 4)
        for copy in copies:
            copy.wait()
        gather(1, halo.at[sweep, 0], 4, 1)
        gather(2, halo.at[sweep, 1], 5, 1)
        for t in range(cells):
            total = rhs[t] + couple[t, 0] * chosen(t, 0) + couple[t, 1] * chosen(t, 1)
            total = total + couple[t, 2] * (chosen(t, 2) + chosen(t, 4))
            right[t] = total + couple[t, 3] * (chosen(t, 3) + chosen(t, 5))

    @pl.when(not_end)
    def _():
        form_right(start, first_halos, 0)

    mats = remote(last, mat_in.at[0], mat_send.at[0], mat_recv.at[0], (inner, surf))
    mats_mid = remote(last, mat_in.at[1], mat_send.at[1], mat_recv.at[1], (inner, surf))

    @pl.when(not_end)
    def _():
        mats.wait_recv()

    @pl.when(depth == 0)
    def _():
        mat_in[0] = jnp.zeros_like(mat_in[0])

    last[...] = mat_in[0]

    edge_step = jnp.where(lower, 0, cells - 1)
    eye = lax.broadcasted_iota(jnp.int32, (width, lines), 0)

    @pl.when(me == 0)
    def _():
        edge_mat[...] = jnp.zeros_like(edge_mat)
        edge_coef[...] = jnp.zeros_like(edge_coef)

    def factor(t, carry):
        for i in range(width):
            win[t, i] = win_own[t, i]
            wout[t, i] = wout_own[t, i]
            diag[t, i] = diag_own[t, i]

        @pl.when(t == edge_step)
        def _():
            @pl.when(me > 0)
            def _():
                for copy in edge_copies:
                    copy.wait_recv()

            for i in range(width):
                diag[t, i] = diag[t, i] + jnp.where(eye == i, edge_coef[...], 0.0)

            @pl.when(lower)
            def _():
                for i in range(width):
                    win[t, i] = edge_mat[i]

            @pl.when(jnp.logical_not(lower))
            def _():
                for i in range(width):
                    wout[t, i] = edge_mat[i]

        product(work, last, win.at[t], diag.at[t])
        dinv[t] = work[...]
        invert_in_place(dinv.at[t])
        product(last, wout.at[t], dinv.at[t])
        coup[t] = last[...]
        return carry

    lax.fori_loop(0, cells, factor, 0)

    @pl.when(jnp.logical_not(is_mid))
    def _():
        mats.start()

    @pl.when(is_mid)
    def _():
        mats_mid.start()
        mats_mid.wait()
        product(mid_inv, mat_in.at[1], wout.at[cells - 1], work)
        invert_in_place(mid_inv)

    for sweep in range(ITERS):
        if sweep == 0:
            @pl.when(depth == 0)
            def _():
                form_right(start, first_halos, 0)
        else:
            copies = halos(prev, sweep)
            for copy in copies:
                copy.start()
            form_right(prev, copies, sweep)

        vec = remote(send_vec, vec_in.at[sweep, 0], vec_send.at[sweep, 0], vec_recv.at[sweep, 0], (inner, surf))
        vec_mid = remote(send_vec, vec_in.at[sweep, 1], vec_send.at[sweep, 1], vec_recv.at[sweep, 1], (inner, surf))

        @pl.when(depth == 0)
        def _():
            vec_in[sweep, 0] = jnp.zeros((width, lines), jnp.float32)

        @pl.when(not_end)
        def _():
            vec.wait_recv()

        send_vec[...] = vec_in[sweep, 0]

        def forward(t, carry):
            rprime[...] = right[t] - matvec(win.at[t], send_vec)
            value = matvec(dinv.at[t], rprime)
            vecs[t] = value
            send_vec[...] = value
            return carry

        lax.fori_loop(0, cells, forward, 0)

        back = remote(vecs.at[0], x_in.at[sweep], x_send.at[sweep], x_recv.at[sweep], (outer, surf))

        @pl.when(jnp.logical_not(is_mid))
        def _():
            vec.start()
            vec.wait_send()
            back.wait_recv()
            vecs[cells - 1] = vecs[cells - 1] - matvec(coup.at[cells - 1], x_in.at[sweep])

        @pl.when(is_mid)
        def _():
            vec_mid.start()
            vec_mid.wait()
            rprime[...] = rprime[...] - matvec(wout.at[cells - 1], vec_in.at[sweep, 1])
            vecs[cells - 1] = matvec(mid_inv, rprime)

        def backward(s, carry):
            t = cells - 2 - s
            vecs[t] = vecs[t] - matvec(coup.at[t], vecs.at[t + 1])
            return carry

        lax.fori_loop(0, cells - 1, backward, 0)

        @pl.when(not_end)
        def _():
            back.start()
            back.wait_send()

        target = out if sweep == ITERS - 1 else prev
        for t in range(cells):
            target[t] = vecs[t]

    @pl.when(me < n_line - 1)
    def _():
        for copy in edge_copies:
            copy.wait_send()

    @pl.when(jnp.logical_not(is_mid))
    def _():
        mats.wait_send()


def on_device(
    face_coef, face_mix, cell_mix, time_term, couple, rhs, start_delta, neighbours, wall_type
):
    cells, width, _, lines = face_mix.shape
    n_line, n_surf = lax.axis_size("line"), lax.axis_size("surf")
    identity = jnp.eye(width, dtype=jnp.float32)[None, :, :, None]
    place = lax.axis_index("line")
    is_first = (place == 0).astype(jnp.float32)
    wall_term = jnp.zeros(wall_type.shape, jnp.float32)
    for wall_kind, wall_value in enumerate(wall_levels):
        wall_term = wall_term + jnp.where(wall_type == wall_kind, wall_value, 0.0)
    coef_diag = face_coef.at[1:].add(face_coef[:-1]).at[0].add(is_first * wall_term)
    extra = time_term + jnp.sum(couple, axis=1) + coef_diag[:, None]
    cell_t = jnp.swapaxes(cell_mix, 1, 2)
    diag_t = identity * extra[:, None] + cell_t - cell_mix
    above_t = -face_coef[:, None, None] * identity - face_mix
    lower_t = jnp.concatenate([jnp.zeros_like(above_t[:1]), above_t[:-1]], 0)
    upper_t = -face_coef[:, None, None] * identity + jnp.swapaxes(face_mix, 1, 2)
    low = place < n_line // 2
    win = jnp.where(low, lower_t, upper_t[::-1])
    wout = jnp.where(low, upper_t, lower_t[::-1])

    def order(array):
        return jnp.where(low, array, array[::-1])

    f32 = jnp.float32
    mat = (width, width, lines)
    pad = (width + 7) // 8 * 8
    vec = (width, lines)
    dma = pltpu.SemaphoreType.DMA
    vmem = pl.BlockSpec(memory_space=pltpu.VMEM)
    solved = pl.pallas_call(
        functools.partial(kernel, n_line, n_surf),
        out_shape=jax.ShapeDtypeStruct((cells,) + vec, f32),
        in_specs=[vmem] * 9,
        out_specs=vmem,
        scratch_shapes=[
            pltpu.VMEM((cells,) + mat, f32),
            pltpu.VMEM((cells,) + mat, f32),
            pltpu.VMEM((cells,) + mat, f32),
            pltpu.VMEM(mat, f32),
            pltpu.VMEM((1, lines), f32),
            dma((2,)), dma((2,)),
            pltpu.VMEM((cells,) + mat, f32),
            pltpu.VMEM((cells,) + mat, f32),
            pltpu.VMEM(mat, f32),
            pltpu.VMEM(mat, f32),
            pltpu.VMEM(mat, f32),
            pltpu.VMEM((2,) + mat, f32),
            pltpu.VMEM((ITERS, 2) + vec, f32),
            pltpu.VMEM((ITERS,) + vec, f32),
            pltpu.VMEM((ITERS, 2, cells) + vec, f32),
            pltpu.VMEM((cells,) + vec, f32),
            pltpu.VMEM((cells,) + vec, f32),
            pltpu.VMEM((cells,) + vec, f32),
            pltpu.VMEM(vec, f32),
            pltpu.VMEM(vec, f32),
            pltpu.VMEM((lines, 6 * lines), f32),
            pltpu.VMEM((3, 3 * cells * pad, lines), f32),
            pltpu.VMEM((3 * cells * pad, 6 * lines), f32),
            dma((2,)), dma((2,)),
            dma((ITERS, 2)), dma((ITERS, 2)),
            dma((ITERS,)), dma((ITERS,)),
            dma((ITERS, 2)), dma((ITERS, 2)),
        ],
        compiler_params=pltpu.CompilerParams(
            collective_id=0, has_side_effects=True, vmem_limit_bytes=40 * 1024 * 1024
        ),
    )(win, wout, order(diag_t), above_t[-1], face_coef[-1:], order(couple), order(rhs), order(start_delta), neighbours)
    return order(solved)


def solution(mesh):
    placed = (
        P("line", "surf"),
        P("line", None, None, "surf"),
        P("line", None, None, "surf"),
        P("line", None, "surf"),
        P("line", None, None, "surf"),
        P("line", None, "surf"),
        P("line", None, "surf"),
        P(None, "surf"),
        P("surf"),
    )
    return jax.shard_map(
        on_device, mesh=mesh, in_specs=placed, out_specs=P("line", None, "surf"), check_vma=False
    )
```

```python
import functools

import jax
import jax.numpy as jnp
from jax import lax
from jax.experimental import pallas as pl
from jax.experimental.pallas import tpu as pltpu
from jax.sharding import PartitionSpec as P

ITERS = 2
MESH = pl.DeviceIdType.MESH

wall_levels = (0.5, 4.0, 32.0)


def groups(width, size=6):
    return [range(s, min(s + size, width)) for s in range(0, width, size)]


def product(out, left, right, base=None):
    width = left.shape[0]
    for rows in groups(width):
        acc = [None] * len(rows)
        for j in range(width):
            line = right[j]
            for n, k in enumerate(rows):
                term = left[k, j : j + 1, :] * line
                acc[n] = term if acc[n] is None else acc[n] + term
        for n, k in enumerate(rows):
            out[k] = acc[n] if base is None else base[k] - acc[n]


def invert_in_place(a):
    width = a.shape[0]
    ids = lax.broadcasted_iota(jnp.int32, a.shape[1:], 0)
    rows = [a[i] for i in range(width)]
    for k in range(width):
        inv = 1.0 / rows[k][k : k + 1, :]
        scaled = rows[k] * inv
        here = ids == k
        update = jnp.where(here, 1.0 + inv, scaled)
        for step in range(1, width):
            i = (k + step) % width
            rows[i] = rows[i] - rows[i][k : k + 1, :] * update
        rows[k] = jnp.where(here, inv, scaled)
    for i in range(width):
        a[i] = rows[i]


def matvec(columns, vector):
    width = columns.shape[0]
    parts = [None] * 3
    for j in range(width):
        term = columns[j] * vector[j : j + 1, :]
        parts[j % 3] = term if parts[j % 3] is None else parts[j % 3] + term
    return parts[0] + parts[1] + parts[2]


def kernel(
    n_line, n_surf,
    win_own, wout_own, diag_own, top_mat, top_coef, couple, rhs, start, neighbours,
    out,
    win, wout, diag, edge_mat, edge_coef, edge_send, edge_recv,
    dinv, coup, last, mid_inv, work, mat_in, vec_in, x_in, halo, prev, vecs, right, rprime, send_vec, onehot, stack, picked,
    mat_send, mat_recv, vec_send, vec_recv, x_send, x_recv, halo_send, halo_recv,
):
    cells, width, _, lines = diag_own.shape
    half = n_line // 2
    rows_each = stack.shape[1] // (3 * cells)
    me = lax.axis_index("line")
    surf = lax.axis_index("surf")
    above = lax.rem(me + 1, n_line)
    below = lax.rem(me + n_line - 1, n_line)
    lower = me < half
    depth = jnp.where(lower, me, n_line - 1 - me)
    inner = jnp.where(lower, me + 1, me - 1)
    outer = jnp.where(lower, lax.rem(me + n_line - 1, n_line), lax.rem(me + 1, n_line))
    is_mid = depth == half - 1
    not_end = depth > 0
    before = lax.rem(surf + n_surf - 1, n_surf)
    after = lax.rem(surf + 1, n_surf)

    barrier = pltpu.get_barrier_semaphore()
    for peer in (above, below):
        pl.semaphore_signal(barrier, inc=1, device_id=(peer, surf), device_id_type=MESH)
    for peer in (before, after):
        pl.semaphore_signal(barrier, inc=1, device_id=(me, peer), device_id_type=MESH)
    pl.semaphore_wait(barrier, 4)

    def remote(src, dst, send, recv, device):
        return pltpu.make_async_remote_copy(
            src_ref=src, dst_ref=dst, send_sem=send, recv_sem=recv,
            device_id=device, device_id_type=MESH,
        )

    def halos(src, sweep):
        return (
            remote(src, halo.at[sweep, 0], halo_send.at[sweep, 0], halo_recv.at[sweep, 0], (me, after)),
            remote(src, halo.at[sweep, 1], halo_send.at[sweep, 1], halo_recv.at[sweep, 1], (me, before)),
        )

    first_halos = halos(start, 0)
    for copy in first_halos:
        copy.start()

    edge_copies = (
        remote(top_mat, edge_mat, edge_send.at[0], edge_recv.at[0], (above, surf)),
        remote(top_coef, edge_coef, edge_send.at[1], edge_recv.at[1], (above, surf)),
    )

    @pl.when(me < n_line - 1)
    def _():
        for copy in edge_copies:
            copy.start()

    source = lax.broadcasted_iota(jnp.int32, (lines, lines), 0)
    own = surf * lines
    for n, (slot, base) in enumerate(
        ((0, own), (1, own), (2, own), (3, own), (2, before * lines), (3, after * lines))
    ):
        hits = neighbours[slot : slot + 1, :] == source + base
        onehot[:, n * lines : (n + 1) * lines] = hits.astype(jnp.float32)
    for which in range(3):
        stack[which] = jnp.zeros_like(stack[which])

    def gather(which, values, first, count):
        pieces = stack.at[which]
        for t in range(cells):
            rest = values[t]
            for q in range(3):
                piece = rest.astype(jnp.bfloat16).astype(jnp.float32)
                begin = (q * cells + t) * rows_each
                pieces[begin : begin + width, :] = piece
                rest = rest - piece
        picked[:, first * lines : (first + count) * lines] = jnp.dot(
            pieces[...].astype(jnp.bfloat16),
            onehot[:, first * lines : (first + count) * lines].astype(jnp.bfloat16),
            preferred_element_type=jnp.float32,
        )

    def chosen(t, n):
        parts = []
        for q in range(3):
            begin = (q * cells + t) * rows_each
            parts.append(picked[begin : begin + width, n * lines : (n + 1) * lines])
        return parts[2] + parts[1] + parts[0]

    def form_right(values, copies, sweep):
        gather(0, values, 0, 4)
        for copy in copies:
            copy.wait()
        gather(1, halo.at[sweep, 0], 4, 1)
        gather(2, halo.at[sweep, 1], 5, 1)
        for t in range(cells):
            total = rhs[t] + couple[t, 0] * chosen(t, 0) + couple[t, 1] * chosen(t, 1)
            total = total + couple[t, 2] * (chosen(t, 2) + chosen(t, 4))
            right[t] = total + couple[t, 3] * (chosen(t, 3) + chosen(t, 5))

    @pl.when(not_end)
    def _():
        form_right(start, first_halos, 0)

    mats = remote(last, mat_in.at[0], mat_send.at[0], mat_recv.at[0], (inner, surf))
    mats_mid = remote(last, mat_in.at[1], mat_send.at[1], mat_recv.at[1], (inner, surf))

    @pl.when(not_end)
    def _():
        mats.wait_recv()

    @pl.when(depth == 0)
    def _():
        mat_in[0] = jnp.zeros_like(mat_in[0])

    last[...] = mat_in[0]

    edge_step = jnp.where(lower, 0, cells - 1)
    eye = lax.broadcasted_iota(jnp.int32, (width, lines), 0)

    @pl.when(me == 0)
    def _():
        edge_mat[...] = jnp.zeros_like(edge_mat)
        edge_coef[...] = jnp.zeros_like(edge_coef)

    def factor(t, carry):
        for i in range(width):
            win[t, i] = win_own[t, i]
            wout[t, i] = wout_own[t, i]
            diag[t, i] = diag_own[t, i]

        @pl.when(t == edge_step)
        def _():
            @pl.when(me > 0)
            def _():
                for copy in edge_copies:
                    copy.wait_recv()

            for i in range(width):
                diag[t, i] = diag[t, i] + jnp.where(eye == i, edge_coef[...], 0.0)

            @pl.when(lower)
            def _():
                for i in range(width):
                    win[t, i] = edge_mat[i]

            @pl.when(jnp.logical_not(lower))
            def _():
                for i in range(width):
                    wout[t, i] = edge_mat[i]

        product(work, last, win.at[t], diag.at[t])
        dinv[t] = work[...]
        invert_in_place(dinv.at[t])
        product(last, wout.at[t], dinv.at[t])
        coup[t] = last[...]
        return carry

    lax.fori_loop(0, cells, factor, 0)

    @pl.when(jnp.logical_not(is_mid))
    def _():
        mats.start()

    @pl.when(is_mid)
    def _():
        mats_mid.start()
        mats_mid.wait()
        product(mid_inv, mat_in.at[1], wout.at[cells - 1], work)
        invert_in_place(mid_inv)

    for sweep in range(ITERS):
        if sweep == 0:
            @pl.when(depth == 0)
            def _():
                form_right(start, first_halos, 0)
        else:
            copies = halos(prev, sweep)
            for copy in copies:
                copy.start()
            form_right(prev, copies, sweep)

        vec = remote(send_vec, vec_in.at[sweep, 0], vec_send.at[sweep, 0], vec_recv.at[sweep, 0], (inner, surf))
        vec_mid = remote(send_vec, vec_in.at[sweep, 1], vec_send.at[sweep, 1], vec_recv.at[sweep, 1], (inner, surf))

        @pl.when(depth == 0)
        def _():
            vec_in[sweep, 0] = jnp.zeros((width, lines), jnp.float32)

        @pl.when(not_end)
        def _():
            vec.wait_recv()

        send_vec[...] = vec_in[sweep, 0]

        def forward(t, carry):
            rprime[...] = right[t] - matvec(win.at[t], send_vec)
            value = matvec(dinv.at[t], rprime)
            vecs[t] = value
            send_vec[...] = value
            return carry

        lax.fori_loop(0, cells, forward, 0, unroll=True)

        back = remote(vecs.at[0], x_in.at[sweep], x_send.at[sweep], x_recv.at[sweep], (outer, surf))

        @pl.when(jnp.logical_not(is_mid))
        def _():
            vec.start()
            vec.wait_send()
            back.wait_recv()
            vecs[cells - 1] = vecs[cells - 1] - matvec(coup.at[cells - 1], x_in.at[sweep])

        @pl.when(is_mid)
        def _():
            vec_mid.start()
            vec_mid.wait()
            rprime[...] = rprime[...] - matvec(wout.at[cells - 1], vec_in.at[sweep, 1])
            vecs[cells - 1] = matvec(mid_inv, rprime)

        def backward(s, carry):
            t = cells - 2 - s
            vecs[t] = vecs[t] - matvec(coup.at[t], vecs.at[t + 1])
            return carry

        lax.fori_loop(0, cells - 1, backward, 0, unroll=True)

        @pl.when(not_end)
        def _():
            back.start()
            back.wait_send()

        target = out if sweep == ITERS - 1 else prev
        for t in range(cells):
            target[t] = vecs[t]

    @pl.when(me < n_line - 1)
    def _():
        for copy in edge_copies:
            copy.wait_send()

    @pl.when(jnp.logical_not(is_mid))
    def _():
        mats.wait_send()


def on_device(
    face_coef, face_mix, cell_mix, time_term, couple, rhs, start_delta, neighbours, wall_type
):
    cells, width, _, lines = face_mix.shape
    n_line, n_surf = lax.axis_size("line"), lax.axis_size("surf")
    identity = jnp.eye(width, dtype=jnp.float32)[None, :, :, None]
    place = lax.axis_index("line")
    is_first = (place == 0).astype(jnp.float32)
    wall_term = jnp.zeros(wall_type.shape, jnp.float32)
    for wall_kind, wall_value in enumerate(wall_levels):
        wall_term = wall_term + jnp.where(wall_type == wall_kind, wall_value, 0.0)
    coef_diag = face_coef.at[1:].add(face_coef[:-1]).at[0].add(is_first * wall_term)
    extra = time_term + jnp.sum(couple, axis=1) + coef_diag[:, None]
    cell_t = jnp.swapaxes(cell_mix, 1, 2)
    diag_t = identity * extra[:, None] + cell_t - cell_mix
    above_t = -face_coef[:, None, None] * identity - face_mix
    lower_t = jnp.concatenate([jnp.zeros_like(above_t[:1]), above_t[:-1]], 0)
    upper_t = -face_coef[:, None, None] * identity + jnp.swapaxes(face_mix, 1, 2)
    low = place < n_line // 2
    win = jnp.where(low, lower_t, upper_t[::-1])
    wout = jnp.where(low, upper_t, lower_t[::-1])

    def order(array):
        return jnp.where(low, array, array[::-1])

    f32 = jnp.float32
    mat = (width, width, lines)
    pad = (width + 7) // 8 * 8
    vec = (width, lines)
    dma = pltpu.SemaphoreType.DMA
    vmem = pl.BlockSpec(memory_space=pltpu.VMEM)
    solved = pl.pallas_call(
        functools.partial(kernel, n_line, n_surf),
        out_shape=jax.ShapeDtypeStruct((cells,) + vec, f32),
        in_specs=[vmem] * 9,
        out_specs=vmem,
        scratch_shapes=[
            pltpu.VMEM((cells,) + mat, f32),
            pltpu.VMEM((cells,) + mat, f32),
            pltpu.VMEM((cells,) + mat, f32),
            pltpu.VMEM(mat, f32),
            pltpu.VMEM((1, lines), f32),
            dma((2,)), dma((2,)),
            pltpu.VMEM((cells,) + mat, f32),
            pltpu.VMEM((cells,) + mat, f32),
            pltpu.VMEM(mat, f32),
            pltpu.VMEM(mat, f32),
            pltpu.VMEM(mat, f32),
            pltpu.VMEM((2,) + mat, f32),
            pltpu.VMEM((ITERS, 2) + vec, f32),
            pltpu.VMEM((ITERS,) + vec, f32),
            pltpu.VMEM((ITERS, 2, cells) + vec, f32),
            pltpu.VMEM((cells,) + vec, f32),
            pltpu.VMEM((cells,) + vec, f32),
            pltpu.VMEM((cells,) + vec, f32),
            pltpu.VMEM(vec, f32),
            pltpu.VMEM(vec, f32),
            pltpu.VMEM((lines, 6 * lines), f32),
            pltpu.VMEM((3, 3 * cells * pad, lines), f32),
            pltpu.VMEM((3 * cells * pad, 6 * lines), f32),
            dma((2,)), dma((2,)),
            dma((ITERS, 2)), dma((ITERS, 2)),
            dma((ITERS,)), dma((ITERS,)),
            dma((ITERS, 2)), dma((ITERS, 2)),
        ],
        compiler_params=pltpu.CompilerParams(
            collective_id=0, has_side_effects=True, vmem_limit_bytes=40 * 1024 * 1024
        ),
    )(win, wout, order(diag_t), above_t[-1], face_coef[-1:], order(couple), order(rhs), order(start_delta), neighbours)
    return order(solved)


def solution(mesh):
    placed = (
        P("line", "surf"),
        P("line", None, None, "surf"),
        P("line", None, None, "surf"),
        P("line", None, "surf"),
        P("line", None, None, "surf"),
        P("line", None, "surf"),
        P("line", None, "surf"),
        P(None, "surf"),
        P("surf"),
    )
    return jax.shard_map(
        on_device, mesh=mesh, in_specs=placed, out_specs=P("line", None, "surf"), check_vma=False
    )
```

```python
import functools

import jax
import jax.numpy as jnp
from jax import lax
from jax.experimental import pallas as pl
from jax.experimental.pallas import tpu as pltpu
from jax.sharding import PartitionSpec as P

ITERS = 2
MESH = pl.DeviceIdType.MESH

wall_levels = (0.5, 4.0, 32.0)


def groups(width, size=6):
    return [range(s, min(s + size, width)) for s in range(0, width, size)]


def product(out, left, right, base=None):
    width = left.shape[0]
    for rows in groups(width):
        acc = [None] * len(rows)
        for j in range(width):
            line = right[j]
            for n, k in enumerate(rows):
                term = left[k, j : j + 1, :] * line
                acc[n] = term if acc[n] is None else acc[n] + term
        for n, k in enumerate(rows):
            out[k] = acc[n] if base is None else base[k] - acc[n]


def invert_in_place(a):
    width = a.shape[0]
    ids = lax.broadcasted_iota(jnp.int32, a.shape[1:], 0)
    rows = [a[i] for i in range(width)]
    for k in range(width):
        inv = 1.0 / rows[k][k : k + 1, :]
        scaled = rows[k] * inv
        here = ids == k
        update = jnp.where(here, 1.0 + inv, scaled)
        for step in range(1, width):
            i = (k + step) % width
            rows[i] = rows[i] - rows[i][k : k + 1, :] * update
        rows[k] = jnp.where(here, inv, scaled)
    for i in range(width):
        a[i] = rows[i]


def matvec(columns, vector):
    width = columns.shape[0]
    parts = [None] * 3
    for j in range(width):
        term = columns[j] * vector[j : j + 1, :]
        parts[j % 3] = term if parts[j % 3] is None else parts[j % 3] + term
    return parts[0] + parts[1] + parts[2]


def kernel(
    n_line, n_surf,
    win_own, wout_own, diag_own, top_mat, top_coef, couple, rhs, start, neighbours,
    out,
    win, wout, diag, step_mat, edge_mat, edge_coef, edge_send, edge_recv,
    dinv, coup, last, mid_inv, work, mat_in, vec_in, x_in, halo, prev, vecs, right, rprime, send_vec, onehot, stack, picked,
    mat_send, mat_recv, vec_send, vec_recv, x_send, x_recv, halo_send, halo_recv,
):
    cells, width, _, lines = diag_own.shape
    half = n_line // 2
    rows_each = stack.shape[1] // (3 * cells)
    me = lax.axis_index("line")
    surf = lax.axis_index("surf")
    above = lax.rem(me + 1, n_line)
    below = lax.rem(me + n_line - 1, n_line)
    lower = me < half
    depth = jnp.where(lower, me, n_line - 1 - me)
    inner = jnp.where(lower, me + 1, me - 1)
    outer = jnp.where(lower, lax.rem(me + n_line - 1, n_line), lax.rem(me + 1, n_line))
    is_mid = depth == half - 1
    not_end = depth > 0
    before = lax.rem(surf + n_surf - 1, n_surf)
    after = lax.rem(surf + 1, n_surf)

    barrier = pltpu.get_barrier_semaphore()
    for peer in (above, below):
        pl.semaphore_signal(barrier, inc=1, device_id=(peer, surf), device_id_type=MESH)
    for peer in (before, after):
        pl.semaphore_signal(barrier, inc=1, device_id=(me, peer), device_id_type=MESH)
    pl.semaphore_wait(barrier, 4)

    def remote(src, dst, send, recv, device):
        return pltpu.make_async_remote_copy(
            src_ref=src, dst_ref=dst, send_sem=send, recv_sem=recv,
            device_id=device, device_id_type=MESH,
        )

    def halos(src, sweep):
        return (
            remote(src, halo.at[sweep, 0], halo_send.at[sweep, 0], halo_recv.at[sweep, 0], (me, after)),
            remote(src, halo.at[sweep, 1], halo_send.at[sweep, 1], halo_recv.at[sweep, 1], (me, before)),
        )

    first_halos = halos(start, 0)
    for copy in first_halos:
        copy.start()

    edge_copies = (
        remote(top_mat, edge_mat, edge_send.at[0], edge_recv.at[0], (above, surf)),
        remote(top_coef, edge_coef, edge_send.at[1], edge_recv.at[1], (above, surf)),
    )

    @pl.when(me < n_line - 1)
    def _():
        for copy in edge_copies:
            copy.start()

    source = lax.broadcasted_iota(jnp.int32, (lines, lines), 0)
    own = surf * lines
    for n, (slot, base) in enumerate(
        ((0, own), (1, own), (2, own), (3, own), (2, before * lines), (3, after * lines))
    ):
        hits = neighbours[slot : slot + 1, :] == source + base
        onehot[:, n * lines : (n + 1) * lines] = hits.astype(jnp.float32)
    for which in range(3):
        stack[which] = jnp.zeros_like(stack[which])

    def gather(which, values, first, count):
        pieces = stack.at[which]
        for t in range(cells):
            rest = values[t]
            for q in range(3):
                piece = rest.astype(jnp.bfloat16).astype(jnp.float32)
                begin = (q * cells + t) * rows_each
                pieces[begin : begin + width, :] = piece
                rest = rest - piece
        picked[:, first * lines : (first + count) * lines] = jnp.dot(
            pieces[...].astype(jnp.bfloat16),
            onehot[:, first * lines : (first + count) * lines].astype(jnp.bfloat16),
            preferred_element_type=jnp.float32,
        )

    def chosen(t, n):
        parts = []
        for q in range(3):
            begin = (q * cells + t) * rows_each
            parts.append(picked[begin : begin + width, n * lines : (n + 1) * lines])
        return parts[2] + parts[1] + parts[0]

    def form_right(values, copies, sweep):
        gather(0, values, 0, 4)
        for copy in copies:
            copy.wait()
        gather(1, halo.at[sweep, 0], 4, 1)
        gather(2, halo.at[sweep, 1], 5, 1)
        for t in range(cells):
            total = rhs[t] + couple[t, 0] * chosen(t, 0) + couple[t, 1] * chosen(t, 1)
            total = total + couple[t, 2] * (chosen(t, 2) + chosen(t, 4))
            right[t] = total + couple[t, 3] * (chosen(t, 3) + chosen(t, 5))

    @pl.when(not_end)
    def _():
        form_right(start, first_halos, 0)

    mats = remote(last, mat_in.at[0], mat_send.at[0], mat_recv.at[0], (inner, surf))
    mats_mid = remote(last, mat_in.at[1], mat_send.at[1], mat_recv.at[1], (inner, surf))

    @pl.when(not_end)
    def _():
        mats.wait_recv()

    @pl.when(depth == 0)
    def _():
        mat_in[0] = jnp.zeros_like(mat_in[0])

    last[...] = mat_in[0]

    edge_step = jnp.where(lower, 0, cells - 1)
    eye = lax.broadcasted_iota(jnp.int32, (width, lines), 0)

    @pl.when(me == 0)
    def _():
        edge_mat[...] = jnp.zeros_like(edge_mat)
        edge_coef[...] = jnp.zeros_like(edge_coef)

    def factor(t, carry):
        for i in range(width):
            win[t, i] = win_own[t, i]
            wout[t, i] = wout_own[t, i]
            diag[t, i] = diag_own[t, i]

        @pl.when(t == edge_step)
        def _():
            @pl.when(me > 0)
            def _():
                for copy in edge_copies:
                    copy.wait_recv()

            for i in range(width):
                diag[t, i] = diag[t, i] + jnp.where(eye == i, edge_coef[...], 0.0)

            @pl.when(lower)
            def _():
                for i in range(width):
                    win[t, i] = edge_mat[i]

            @pl.when(jnp.logical_not(lower))
            def _():
                for i in range(width):
                    wout[t, i] = edge_mat[i]

        product(work, last, win.at[t], diag.at[t])
        dinv[t] = work[...]
        invert_in_place(dinv.at[t])
        product(last, wout.at[t], dinv.at[t])
        coup[t] = last[...]
        return carry

    lax.fori_loop(0, cells, factor, 0)

    @pl.when(jnp.logical_not(is_mid))
    def _():
        mats.start()

    @pl.when(is_mid)
    def _():
        mats_mid.start()

    def chain(t, carry):
        product(step_mat.at[t], win.at[t], dinv.at[t])
        return carry

    lax.fori_loop(0, cells, chain, 0)

    @pl.when(is_mid)
    def _():
        mats_mid.wait()
        product(mid_inv, mat_in.at[1], wout.at[cells - 1], work)
        invert_in_place(mid_inv)

    for sweep in range(ITERS):
        if sweep == 0:
            @pl.when(depth == 0)
            def _():
                form_right(start, first_halos, 0)
        else:
            copies = halos(prev, sweep)
            for copy in copies:
                copy.start()
            form_right(prev, copies, sweep)

        vec = remote(send_vec, vec_in.at[sweep, 0], vec_send.at[sweep, 0], vec_recv.at[sweep, 0], (inner, surf))
        vec_mid = remote(send_vec, vec_in.at[sweep, 1], vec_send.at[sweep, 1], vec_recv.at[sweep, 1], (inner, surf))

        for t in range(cells):
            vecs[t] = matvec(dinv.at[t], right.at[t])

        @pl.when(depth == 0)
        def _():
            vec_in[sweep, 0] = jnp.zeros((width, lines), jnp.float32)

        @pl.when(not_end)
        def _():
            vec.wait_recv()

        for t in range(cells):
            prior = vecs.at[t - 1] if t else vec_in.at[sweep, 0]
            vecs[t] = vecs[t] - matvec(step_mat.at[t], prior)
        send_vec[...] = vecs[cells - 1]

        back = remote(vecs.at[0], x_in.at[sweep], x_send.at[sweep], x_recv.at[sweep], (outer, surf))

        @pl.when(jnp.logical_not(is_mid))
        def _():
            vec.start()
            vec.wait_send()
            back.wait_recv()
            vecs[cells - 1] = vecs[cells - 1] - matvec(coup.at[cells - 1], x_in.at[sweep])

        @pl.when(is_mid)
        def _():
            vec_mid.start()
            prior = vecs.at[cells - 2] if cells > 1 else vec_in.at[sweep, 0]
            rprime[...] = right[cells - 1] - matvec(win.at[cells - 1], prior)
            vec_mid.wait()
            rprime[...] = rprime[...] - matvec(wout.at[cells - 1], vec_in.at[sweep, 1])
            vecs[cells - 1] = matvec(mid_inv, rprime)

        def backward(s, carry):
            t = cells - 2 - s
            vecs[t] = vecs[t] - matvec(coup.at[t], vecs.at[t + 1])
            return carry

        lax.fori_loop(0, cells - 1, backward, 0)

        @pl.when(not_end)
        def _():
            back.start()
            back.wait_send()

        target = out if sweep == ITERS - 1 else prev
        for t in range(cells):
            target[t] = vecs[t]

    @pl.when(me < n_line - 1)
    def _():
        for copy in edge_copies:
            copy.wait_send()

    @pl.when(jnp.logical_not(is_mid))
    def _():
        mats.wait_send()


def on_device(
    face_coef, face_mix, cell_mix, time_term, couple, rhs, start_delta, neighbours, wall_type
):
    cells, width, _, lines = face_mix.shape
    n_line, n_surf = lax.axis_size("line"), lax.axis_size("surf")
    identity = jnp.eye(width, dtype=jnp.float32)[None, :, :, None]
    place = lax.axis_index("line")
    is_first = (place == 0).astype(jnp.float32)
    wall_term = jnp.zeros(wall_type.shape, jnp.float32)
    for wall_kind, wall_value in enumerate(wall_levels):
        wall_term = wall_term + jnp.where(wall_type == wall_kind, wall_value, 0.0)
    coef_diag = face_coef.at[1:].add(face_coef[:-1]).at[0].add(is_first * wall_term)
    extra = time_term + jnp.sum(couple, axis=1) + coef_diag[:, None]
    cell_t = jnp.swapaxes(cell_mix, 1, 2)
    diag_t = identity * extra[:, None] + cell_t - cell_mix
    above_t = -face_coef[:, None, None] * identity - face_mix
    lower_t = jnp.concatenate([jnp.zeros_like(above_t[:1]), above_t[:-1]], 0)
    upper_t = -face_coef[:, None, None] * identity + jnp.swapaxes(face_mix, 1, 2)
    low = place < n_line // 2
    win = jnp.where(low, lower_t, upper_t[::-1])
    wout = jnp.where(low, upper_t, lower_t[::-1])

    def order(array):
        return jnp.where(low, array, array[::-1])

    f32 = jnp.float32
    mat = (width, width, lines)
    pad = (width + 7) // 8 * 8
    vec = (width, lines)
    dma = pltpu.SemaphoreType.DMA
    vmem = pl.BlockSpec(memory_space=pltpu.VMEM)
    solved = pl.pallas_call(
        functools.partial(kernel, n_line, n_surf),
        out_shape=jax.ShapeDtypeStruct((cells,) + vec, f32),
        in_specs=[vmem] * 9,
        out_specs=vmem,
        scratch_shapes=[
            pltpu.VMEM((cells,) + mat, f32),
            pltpu.VMEM((cells,) + mat, f32),
            pltpu.VMEM((cells,) + mat, f32),
            pltpu.VMEM((cells,) + mat, f32),
            pltpu.VMEM(mat, f32),
            pltpu.VMEM((1, lines), f32),
            dma((2,)), dma((2,)),
            pltpu.VMEM((cells,) + mat, f32),
            pltpu.VMEM((cells,) + mat, f32),
            pltpu.VMEM(mat, f32),
            pltpu.VMEM(mat, f32),
            pltpu.VMEM(mat, f32),
            pltpu.VMEM((2,) + mat, f32),
            pltpu.VMEM((ITERS, 2) + vec, f32),
            pltpu.VMEM((ITERS,) + vec, f32),
            pltpu.VMEM((ITERS, 2, cells) + vec, f32),
            pltpu.VMEM((cells,) + vec, f32),
            pltpu.VMEM((cells,) + vec, f32),
            pltpu.VMEM((cells,) + vec, f32),
            pltpu.VMEM(vec, f32),
            pltpu.VMEM(vec, f32),
            pltpu.VMEM((lines, 6 * lines), f32),
            pltpu.VMEM((3, 3 * cells * pad, lines), f32),
            pltpu.VMEM((3 * cells * pad, 6 * lines), f32),
            dma((2,)), dma((2,)),
            dma((ITERS, 2)), dma((ITERS, 2)),
            dma((ITERS,)), dma((ITERS,)),
            dma((ITERS, 2)), dma((ITERS, 2)),
        ],
        compiler_params=pltpu.CompilerParams(
            collective_id=0, has_side_effects=True, vmem_limit_bytes=40 * 1024 * 1024
        ),
    )(win, wout, order(diag_t), above_t[-1], face_coef[-1:], order(couple), order(rhs), order(start_delta), neighbours)
    return order(solved)


def solution(mesh):
    placed = (
        P("line", "surf"),
        P("line", None, None, "surf"),
        P("line", None, None, "surf"),
        P("line", None, "surf"),
        P("line", None, None, "surf"),
        P("line", None, "surf"),
        P("line", None, "surf"),
        P(None, "surf"),
        P("surf"),
    )
    return jax.shard_map(
        on_device, mesh=mesh, in_specs=placed, out_specs=P("line", None, "surf"), check_vma=False
    )
```

```python
import functools

import jax
import jax.numpy as jnp
from jax import lax
from jax.experimental import pallas as pl
from jax.experimental.pallas import tpu as pltpu
from jax.sharding import PartitionSpec as P

ITERS = 2
MESH = pl.DeviceIdType.MESH

wall_levels = (0.5, 4.0, 32.0)


def groups(width, size=6):
    return [range(s, min(s + size, width)) for s in range(0, width, size)]


def product(out, left, right, base=None):
    width = left.shape[0]
    for rows in groups(width):
        acc = [None] * len(rows)
        for j in range(width):
            line = right[j]
            for n, k in enumerate(rows):
                term = left[k, j : j + 1, :] * line
                acc[n] = term if acc[n] is None else acc[n] + term
        for n, k in enumerate(rows):
            out[k] = acc[n] if base is None else base[k] - acc[n]


def invert_in_place(a):
    width = a.shape[0]
    ids = lax.broadcasted_iota(jnp.int32, a.shape[1:], 0)
    rows = [a[i] for i in range(width)]
    for k in range(width):
        inv = 1.0 / rows[k][k : k + 1, :]
        scaled = rows[k] * inv
        here = ids == k
        update = jnp.where(here, 1.0 + inv, scaled)
        for step in range(1, width):
            i = (k + step) % width
            rows[i] = rows[i] - rows[i][k : k + 1, :] * update
        rows[k] = jnp.where(here, inv, scaled)
    for i in range(width):
        a[i] = rows[i]


def matvec(columns, vector):
    width = columns.shape[0]
    parts = [None] * 3
    for j in range(width):
        term = columns[j] * vector[j : j + 1, :]
        parts[j % 3] = term if parts[j % 3] is None else parts[j % 3] + term
    return parts[0] + parts[1] + parts[2]


def kernel(
    n_line, n_surf,
    win_own, wout_own, diag_own, top_mat, top_coef, couple, rhs, start, neighbours,
    out,
    win, wout, diag, step_mat, edge_mat, edge_coef, edge_send, edge_recv,
    dinv, coup, last, mid_inv, work, mat_in, vec_in, x_in, halo, prev, vecs, right, rprime, send_vec, send_back, onehot, stack, picked,
    mat_send, mat_recv, vec_send, vec_recv, x_send, x_recv, halo_send, halo_recv,
):
    cells, width, _, lines = diag_own.shape
    half = n_line // 2
    rows_each = stack.shape[1] // (3 * cells)
    me = lax.axis_index("line")
    surf = lax.axis_index("surf")
    above = lax.rem(me + 1, n_line)
    below = lax.rem(me + n_line - 1, n_line)
    lower = me < half
    depth = jnp.where(lower, me, n_line - 1 - me)
    inner = jnp.where(lower, me + 1, me - 1)
    outer = jnp.where(lower, lax.rem(me + n_line - 1, n_line), lax.rem(me + 1, n_line))
    is_mid = depth == half - 1
    not_end = depth > 0
    before = lax.rem(surf + n_surf - 1, n_surf)
    after = lax.rem(surf + 1, n_surf)

    barrier = pltpu.get_barrier_semaphore()
    for peer in (above, below):
        pl.semaphore_signal(barrier, inc=1, device_id=(peer, surf), device_id_type=MESH)
    for peer in (before, after):
        pl.semaphore_signal(barrier, inc=1, device_id=(me, peer), device_id_type=MESH)
    pl.semaphore_wait(barrier, 4)

    def remote(src, dst, send, recv, device):
        return pltpu.make_async_remote_copy(
            src_ref=src, dst_ref=dst, send_sem=send, recv_sem=recv,
            device_id=device, device_id_type=MESH,
        )

    def halos(src, sweep):
        return (
            remote(src, halo.at[sweep, 0], halo_send.at[sweep, 0], halo_recv.at[sweep, 0], (me, after)),
            remote(src, halo.at[sweep, 1], halo_send.at[sweep, 1], halo_recv.at[sweep, 1], (me, before)),
        )

    first_halos = halos(start, 0)
    for copy in first_halos:
        copy.start()

    edge_copies = (
        remote(top_mat, edge_mat, edge_send.at[0], edge_recv.at[0], (above, surf)),
        remote(top_coef, edge_coef, edge_send.at[1], edge_recv.at[1], (above, surf)),
    )

    @pl.when(me < n_line - 1)
    def _():
        for copy in edge_copies:
            copy.start()

    source = lax.broadcasted_iota(jnp.int32, (lines, lines), 0)
    own = surf * lines
    for n, (slot, base) in enumerate(
        ((0, own), (1, own), (2, own), (3, own), (2, before * lines), (3, after * lines))
    ):
        hits = neighbours[slot : slot + 1, :] == source + base
        onehot[:, n * lines : (n + 1) * lines] = hits.astype(jnp.float32)
    send_vec[...] = jnp.zeros_like(send_vec)
    send_back[...] = jnp.zeros_like(send_back)
    for which in range(3):
        stack[which] = jnp.zeros_like(stack[which])

    def gather(which, values, first, count):
        pieces = stack.at[which]
        for t in range(cells):
            rest = values[t]
            for q in range(3):
                piece = rest.astype(jnp.bfloat16).astype(jnp.float32)
                begin = (q * cells + t) * rows_each
                pieces[begin : begin + width, :] = piece
                rest = rest - piece
        picked[:, first * lines : (first + count) * lines] = jnp.dot(
            pieces[...].astype(jnp.bfloat16),
            onehot[:, first * lines : (first + count) * lines].astype(jnp.bfloat16),
            preferred_element_type=jnp.float32,
        )

    def chosen(t, n):
        parts = []
        for q in range(3):
            begin = (q * cells + t) * rows_each
            parts.append(picked[begin : begin + width, n * lines : (n + 1) * lines])
        return parts[2] + parts[1] + parts[0]

    def form_right(values, copies, sweep):
        gather(0, values, 0, 4)
        for copy in copies:
            copy.wait()
        gather(1, halo.at[sweep, 0], 4, 1)
        gather(2, halo.at[sweep, 1], 5, 1)
        for t in range(cells):
            total = rhs[t] + couple[t, 0] * chosen(t, 0) + couple[t, 1] * chosen(t, 1)
            total = total + couple[t, 2] * (chosen(t, 2) + chosen(t, 4))
            right[t] = total + couple[t, 3] * (chosen(t, 3) + chosen(t, 5))

    @pl.when(not_end)
    def _():
        form_right(start, first_halos, 0)

    mats = remote(last, mat_in.at[0], mat_send.at[0], mat_recv.at[0], (inner, surf))
    mats_mid = remote(last, mat_in.at[1], mat_send.at[1], mat_recv.at[1], (inner, surf))

    @pl.when(not_end)
    def _():
        mats.wait_recv()

    @pl.when(depth == 0)
    def _():
        mat_in[0] = jnp.zeros_like(mat_in[0])

    last[...] = mat_in[0]

    edge_step = jnp.where(lower, 0, cells - 1)
    eye = lax.broadcasted_iota(jnp.int32, (width, lines), 0)

    @pl.when(me == 0)
    def _():
        edge_mat[...] = jnp.zeros_like(edge_mat)
        edge_coef[...] = jnp.zeros_like(edge_coef)

    def factor(t, carry):
        for i in range(width):
            win[t, i] = win_own[t, i]
            wout[t, i] = wout_own[t, i]
            diag[t, i] = diag_own[t, i]

        @pl.when(t == edge_step)
        def _():
            @pl.when(me > 0)
            def _():
                for copy in edge_copies:
                    copy.wait_recv()

            for i in range(width):
                diag[t, i] = diag[t, i] + jnp.where(eye == i, edge_coef[...], 0.0)

            @pl.when(lower)
            def _():
                for i in range(width):
                    win[t, i] = edge_mat[i]

            @pl.when(jnp.logical_not(lower))
            def _():
                for i in range(width):
                    wout[t, i] = edge_mat[i]

        product(work, last, win.at[t], diag.at[t])
        dinv[t] = work[...]
        invert_in_place(dinv.at[t])
        product(last, wout.at[t], dinv.at[t])
        coup[t] = last[...]
        return carry

    lax.fori_loop(0, cells, factor, 0)

    @pl.when(jnp.logical_not(is_mid))
    def _():
        mats.start()

    @pl.when(is_mid)
    def _():
        mats_mid.start()

    def chain(t, carry):
        product(step_mat.at[t], win.at[t], dinv.at[t])
        return carry

    lax.fori_loop(0, cells, chain, 0)

    @pl.when(is_mid)
    def _():
        mats_mid.wait()
        product(mid_inv, mat_in.at[1], wout.at[cells - 1], work)
        invert_in_place(mid_inv)

    for sweep in range(ITERS):
        if sweep == 0:
            @pl.when(depth == 0)
            def _():
                form_right(start, first_halos, 0)
        else:
            copies = halos(prev, sweep)
            for copy in copies:
                copy.start()
            form_right(prev, copies, sweep)

        vec = remote(send_vec, vec_in.at[sweep, 0], vec_send.at[sweep, 0], vec_recv.at[sweep, 0], (inner, surf))
        vec_mid = remote(send_vec, vec_in.at[sweep, 1], vec_send.at[sweep, 1], vec_recv.at[sweep, 1], (inner, surf))

        for t in range(cells):
            vecs[t] = matvec(dinv.at[t], right.at[t])

        @pl.when(depth == 0)
        def _():
            vec_in[sweep, 0] = jnp.zeros(vec_in.shape[2:], jnp.float32)

        @pl.when(not_end)
        def _():
            vec.wait_recv()

        for t in range(cells):
            prior = vecs.at[t - 1] if t else vec_in.at[sweep, 0]
            vecs[t] = vecs[t] - matvec(step_mat.at[t], prior)
        send_vec[0:width, :] = vecs[cells - 1]

        back = remote(send_back, x_in.at[sweep], x_send.at[sweep], x_recv.at[sweep], (outer, surf))

        @pl.when(jnp.logical_not(is_mid))
        def _():
            vec.start()
            vec.wait_send()
            back.wait_recv()
            vecs[cells - 1] = vecs[cells - 1] - matvec(coup.at[cells - 1], x_in.at[sweep])

        @pl.when(is_mid)
        def _():
            vec_mid.start()
            prior = vecs.at[cells - 2] if cells > 1 else vec_in.at[sweep, 0]
            rprime[...] = right[cells - 1] - matvec(win.at[cells - 1], prior)
            vec_mid.wait()
            rprime[...] = rprime[...] - matvec(wout.at[cells - 1], vec_in.at[sweep, 1])
            vecs[cells - 1] = matvec(mid_inv, rprime)

        def backward(s, carry):
            t = cells - 2 - s
            vecs[t] = vecs[t] - matvec(coup.at[t], vecs.at[t + 1])
            return carry

        lax.fori_loop(0, cells - 1, backward, 0)

        @pl.when(not_end)
        def _():
            send_back[0:width, :] = vecs[0]
            back.start()
            back.wait_send()

        target = out if sweep == ITERS - 1 else prev
        for t in range(cells):
            target[t] = vecs[t]

    @pl.when(me < n_line - 1)
    def _():
        for copy in edge_copies:
            copy.wait_send()

    @pl.when(jnp.logical_not(is_mid))
    def _():
        mats.wait_send()


def on_device(
    face_coef, face_mix, cell_mix, time_term, couple, rhs, start_delta, neighbours, wall_type
):
    cells, width, _, lines = face_mix.shape
    n_line, n_surf = lax.axis_size("line"), lax.axis_size("surf")
    identity = jnp.eye(width, dtype=jnp.float32)[None, :, :, None]
    place = lax.axis_index("line")
    is_first = (place == 0).astype(jnp.float32)
    wall_term = jnp.zeros(wall_type.shape, jnp.float32)
    for wall_kind, wall_value in enumerate(wall_levels):
        wall_term = wall_term + jnp.where(wall_type == wall_kind, wall_value, 0.0)
    coef_diag = face_coef.at[1:].add(face_coef[:-1]).at[0].add(is_first * wall_term)
    extra = time_term + jnp.sum(couple, axis=1) + coef_diag[:, None]
    cell_t = jnp.swapaxes(cell_mix, 1, 2)
    diag_t = identity * extra[:, None] + cell_t - cell_mix
    above_t = -face_coef[:, None, None] * identity - face_mix
    lower_t = jnp.concatenate([jnp.zeros_like(above_t[:1]), above_t[:-1]], 0)
    upper_t = -face_coef[:, None, None] * identity + jnp.swapaxes(face_mix, 1, 2)
    low = place < n_line // 2
    win = jnp.where(low, lower_t, upper_t[::-1])
    wout = jnp.where(low, upper_t, lower_t[::-1])

    def order(array):
        return jnp.where(low, array, array[::-1])

    f32 = jnp.float32
    mat = (width, width, lines)
    pad = (width + 7) // 8 * 8
    vec = (width, lines)
    dma = pltpu.SemaphoreType.DMA
    vmem = pl.BlockSpec(memory_space=pltpu.VMEM)
    solved = pl.pallas_call(
        functools.partial(kernel, n_line, n_surf),
        out_shape=jax.ShapeDtypeStruct((cells,) + vec, f32),
        in_specs=[vmem] * 9,
        out_specs=vmem,
        scratch_shapes=[
            pltpu.VMEM((cells,) + mat, f32),
            pltpu.VMEM((cells,) + mat, f32),
            pltpu.VMEM((cells,) + mat, f32),
            pltpu.VMEM((cells,) + mat, f32),
            pltpu.VMEM(mat, f32),
            pltpu.VMEM((1, lines), f32),
            dma((2,)), dma((2,)),
            pltpu.VMEM((cells,) + mat, f32),
            pltpu.VMEM((cells,) + mat, f32),
            pltpu.VMEM(mat, f32),
            pltpu.VMEM(mat, f32),
            pltpu.VMEM(mat, f32),
            pltpu.VMEM((2,) + mat, f32),
            pltpu.VMEM((ITERS, 2, pad, lines), f32),
            pltpu.VMEM((ITERS, pad, lines), f32),
            pltpu.VMEM((ITERS, 2, cells) + vec, f32),
            pltpu.VMEM((cells,) + vec, f32),
            pltpu.VMEM((cells,) + vec, f32),
            pltpu.VMEM((cells,) + vec, f32),
            pltpu.VMEM(vec, f32),
            pltpu.VMEM((pad, lines), f32),
            pltpu.VMEM((pad, lines), f32),
            pltpu.VMEM((lines, 6 * lines), f32),
            pltpu.VMEM((3, 3 * cells * pad, lines), f32),
            pltpu.VMEM((3 * cells * pad, 6 * lines), f32),
            dma((2,)), dma((2,)),
            dma((ITERS, 2)), dma((ITERS, 2)),
            dma((ITERS,)), dma((ITERS,)),
            dma((ITERS, 2)), dma((ITERS, 2)),
        ],
        compiler_params=pltpu.CompilerParams(
            collective_id=0, has_side_effects=True, vmem_limit_bytes=40 * 1024 * 1024
        ),
    )(win, wout, order(diag_t), above_t[-1], face_coef[-1:], order(couple), order(rhs), order(start_delta), neighbours)
    return order(solved)


def solution(mesh):
    placed = (
        P("line", "surf"),
        P("line", None, None, "surf"),
        P("line", None, None, "surf"),
        P("line", None, "surf"),
        P("line", None, None, "surf"),
        P("line", None, "surf"),
        P("line", None, "surf"),
        P(None, "surf"),
        P("surf"),
    )
    return jax.shard_map(
        on_device, mesh=mesh, in_specs=placed, out_specs=P("line", None, "surf"), check_vma=False
    )
```
